32 devices in a mesh: groups: 2 (over x), blk: 16 (over z, y, core).
Axes of the slice: x: 2, y: 2, z: 4, core: 2. Of those that a mesh axis runs over, the one named last changes fastest.
Arguments:
- tokens: bfloat16 [3072, 16384], P('groups', 'blk'), parts along dimension 0, may hold values from -640 to 640, as said below
- norm_gain: bfloat16 [16384], P('blk'), may hold values from 0.099609375 to 1.8984375
- left_factor: bfloat16 [128, 128, 128], P('blk'), may hold values from -0.5 to 0.5
- right_factor: bfloat16 [128, 128, 128], P('blk'), may hold values from -0.5 to 0.5
- cotangent: bfloat16 [3072, 16384], P('groups', 'blk'), parts along dimension 0, may hold values from -6 to 6
Outputs:
- mixer_out: bfloat16 [3072, 16384], P('groups', 'blk'), parts along dimension 0
- grad_tokens: bfloat16 [3072, 16384], P('groups', 'blk'), parts along dimension 0
- grad_left: float32 [256, 128, 128], P(('groups', 'blk')), parts along dimension 0
- grad_right: float32 [256, 128, 128], P(('groups', 'blk')), parts along dimension 0
- grad_gain: float32 [32768], P(('groups', 'blk')), parts along dimension 0
The draws below stay inside these ranges and needn't reach their ends.
There are 2 independent parts, one for each index of `groups`. The reference program is written for one: setup_inputs(seed, part) draws one part's arguments, and reference() takes and returns one part's arrays. A program takes and returns all parts, laid end to end along the dimension named above; an argument that names none is the same for every part. Nothing has to cross between parts.
Inputs may be any that keep to these rules, and one draw needn't show every extreme that they name: `tokens`: Real-valued activations.
All inputs are finite; a program needn't handle non-finite values.
Results may differ from the reference program's by a relative error of at most 0.0067.
Values may be sent and summed in bfloat16 or wider, within the bound.
A program may use at most 64 MiB of HBM per device.

```python
import math
import jax
import jax.numpy as jnp
from jax import lax

NB = 128
BS = 128
TOK = 1536
D = 16384


def draw_tokens(key, part):
    key_base, key_rows, key_cols = jax.random.split(key, 3)
    position = jnp.arange(D, dtype=jnp.float32)[None, :] / D
    base_values = jax.random.truncated_normal(key_base, -6.0, 6.0, (TOK, D), jnp.float32)
    row_scale = jnp.exp(jax.random.uniform(key_rows, (TOK, 1), jnp.float32, 0.0, math.log(10.0)))
    col_scale = jnp.power(10.0, jax.random.uniform(key_cols, (1, D), jnp.float32) - 0.5) * jnp.power(3.0, position - 0.5)
    return (base_values * row_scale * col_scale).astype(jnp.bfloat16)


def block_levels(stream_key, shape, cuts, low, top_value):
    level = 1.0
    for dim, shards_of in cuts:
        steps = jax.random.uniform(jax.random.fold_in(jax.random.fold_in(stream_key, 6), dim), (shards_of,), jnp.float32, low / len(cuts), top_value / len(cuts))
        level = level * jnp.repeat(jnp.exp(steps), shape[dim] // shards_of).reshape((-1,) + (1,) * (len(shape) - 1 - dim))
    return level


def noise(rng, shape, deviation, reach, cuts=(), kind=jnp.bfloat16):
    factor_of = block_levels(rng, shape, cuts, -0.22, 0.18) if cuts else 1.0
    array = jax.random.normal(rng, shape, jnp.float32) * deviation * factor_of
    return jnp.minimum(jnp.maximum(array, -reach), reach).astype(kind)


def setup_inputs(seed: int = 0, part: int = 0) -> dict:
    key_of = jax.random.split(jax.random.key(seed), 6)
    own_keys = jax.random.split(jax.random.fold_in(key_of[5], part), 6)
    return {
        "tokens": draw_tokens(jax.random.fold_in(jax.random.fold_in(key_of[5], part), 71), part),
        "norm_gain": jnp.clip(1.0 + 0.18 * jax.random.normal(key_of[1], (D,), jnp.float32), 0.099609375, 1.8984375).astype(jnp.bfloat16),
        "left_factor": noise(key_of[2], (NB, BS, BS), BS ** -0.5, 0.5, ((0, 16),)),
        "right_factor": noise(key_of[3], (BS, NB, NB), NB ** -0.5, 0.5, ((0, 16),)),
        "cotangent": noise(own_keys[4], (TOK, D), 1.0, 6.0, ((1, 16),)),
    }


epsilon = 1e-06

def gelu_slope(inputs_f):
    return 0.5 * (1.0 + lax.erf(inputs_f * 0.7071067811865476)) + inputs_f * jnp.exp(-0.5 * inputs_f * inputs_f) * 0.3989422804014327

def reference(tokens, norm_gain, left_factor, right_factor, cotangent):
    widened = tokens.astype(jnp.float32)
    inverse_rms = lax.rsqrt(lax.optimization_barrier(jnp.sum(widened * widened, axis=1)) / D + epsilon)
    gain_wide = norm_gain.astype(jnp.float32)
    normed = (widened * inverse_rms[:, None] * gain_wide[None, :]).astype(jnp.bfloat16)
    blocks = normed.reshape(TOK, NB, BS).astype(jnp.float32)
    left_wide = left_factor.astype(jnp.float32)
    right_wide = right_factor.astype(jnp.float32)
    pre_act = jnp.einsum('tbi,bij->tjb', blocks, left_wide).astype(jnp.bfloat16)
    active = jax.nn.gelu(pre_act.astype(jnp.float32), approximate=False).astype(jnp.bfloat16)
    active_wide = active.astype(jnp.float32)
    mixed_out = jnp.einsum('tjb,jbc->tjc', active_wide, right_wide).astype(jnp.bfloat16)
    mixer_out = jnp.transpose(mixed_out, (0, 2, 1)).reshape(TOK, D)
    grad_mixed = jnp.transpose(cotangent.reshape(TOK, NB, BS), (0, 2, 1)).astype(jnp.float32)
    grad_right = jnp.einsum('tjb,tjc->jbc', active_wide, grad_mixed)
    grad_act = jnp.einsum('tjc,jbc->tjb', grad_mixed, right_wide)
    grad_pre = (grad_act * gelu_slope(pre_act.astype(jnp.float32))).astype(jnp.bfloat16)
    grad_pre_wide = grad_pre.astype(jnp.float32)
    grad_left = jnp.einsum('tbi,tjb->bij', blocks, grad_pre_wide)
    grad_normed = jnp.einsum('tjb,bij->tbi', grad_pre_wide, left_wide).reshape(TOK, D)
    grad_gain = lax.optimization_barrier(jnp.sum(grad_normed * widened * inverse_rms[:, None], axis=0))
    scaled = grad_normed * gain_wide[None, :]
    correction = lax.optimization_barrier(jnp.sum(scaled * widened, axis=1))
    grad_tokens = (inverse_rms[:, None] * scaled - widened * (inverse_rms ** 3 * correction / D)[:, None]).astype(jnp.bfloat16)
    return (mixer_out, grad_tokens, grad_left, grad_right, grad_gain)
```

```python
import jax
import jax.numpy as jnp
from jax import lax
from jax.experimental import pallas as pl
from jax.experimental.pallas import tpu as pltpu
from jax.sharding import PartitionSpec as P

CHUNK = 256


epsilon = 1e-06


def gelu_slope(inputs_f):
    return (
        0.5 * (1.0 + lax.erf(inputs_f * 0.7071067811865476))
        + inputs_f * jnp.exp(-0.5 * inputs_f * inputs_f) * 0.3989422804014327
    )


def on_device(width, tokens, norm_gain, left_factor, right_factor, cotangent):
    row_count = tokens.shape[0]
    local_blocks = left_factor.shape[0]
    block_order = left_factor.shape[1]
    widened = tokens.astype(jnp.float32)
    square_sum = lax.psum(jnp.sum(widened * widened, axis=1), "blk")
    inverse_rms = lax.rsqrt(square_sum / width + epsilon)
    gain_wide = norm_gain.astype(jnp.float32)
    normed = (widened * inverse_rms[:, None] * gain_wide[None, :]).astype(jnp.bfloat16)
    blocks = normed.reshape(row_count, local_blocks, block_order)
    pre_act = jnp.einsum(
        "tbi,bij->btj", blocks, left_factor, preferred_element_type=jnp.float32
    ).astype(jnp.bfloat16)
    pre_piece = lax.all_to_all(pre_act, "blk", split_axis=2, concat_axis=0, tiled=True)
    active = jax.nn.gelu(pre_piece.astype(jnp.float32), approximate=False).astype(jnp.bfloat16)
    mixed_out = jnp.einsum(
        "btj,jbc->jtc", active, right_factor, preferred_element_type=jnp.float32
    ).astype(jnp.bfloat16)
    mixed_out = lax.all_to_all(mixed_out, "blk", split_axis=2, concat_axis=0, tiled=True)
    incoming = jnp.transpose(cotangent.reshape(row_count, -1, block_order), (1, 0, 2))
    grad_mixed = lax.all_to_all(incoming, "blk", split_axis=2, concat_axis=0, tiled=True)
    mixer_out = jnp.transpose(mixed_out, (1, 2, 0)).reshape(row_count, -1)
    grad_right = jnp.einsum("btj,ctj->jbc", active, grad_mixed, preferred_element_type=jnp.float32)
    grad_act = jnp.einsum(
        "ctj,jbc->btj", grad_mixed, right_factor, preferred_element_type=jnp.float32
    )
    grad_pre = (grad_act * gelu_slope(pre_piece.astype(jnp.float32))).astype(jnp.bfloat16)
    grad_back = lax.all_to_all(grad_pre, "blk", split_axis=0, concat_axis=2, tiled=True)
    grad_left = jnp.einsum("tbi,btj->bij", blocks, grad_back, preferred_element_type=jnp.float32)
    grad_normed = jnp.einsum(
        "btj,bij->tbi", grad_back, left_factor, preferred_element_type=jnp.float32
    ).reshape(row_count, -1)
    grad_gain = jnp.sum(grad_normed * widened * inverse_rms[:, None], axis=0)
    scaled = grad_normed * gain_wide[None, :]
    correction = lax.psum(jnp.sum(scaled * widened, axis=1), "blk")
    grad_tokens = (
        inverse_rms[:, None] * scaled - widened * (inverse_rms**3 * correction / width)[:, None]
    ).astype(jnp.bfloat16)
    return (mixer_out, grad_tokens, grad_left, grad_right, grad_gain)

def fast(n, width, tokens, norm_gain, left_factor, right_factor, cotangent):
    rows = tokens.shape[0]
    feats = tokens.shape[1]
    local, order = left_factor.shape[0], left_factor.shape[1]
    piece = local * local
    lg = local.bit_length() - 1
    low = local - 1
    tc = CHUNK
    chunks = rows // tc
    strips = rows // 128
    f32, bf16 = jnp.float32, jnp.bfloat16
    part = 256
    pieces_in_part = part // piece

    def nn(a, b):
        return lax.dot_general(a, b, (((1,), (0,)), ((), ())), preferred_element_type=f32)

    def nt(a, b):
        return lax.dot_general(a, b, (((1,), (1,)), ((), ())), preferred_element_type=f32)

    def tn(a, b):
        return lax.dot_general(a, b, (((0,), (0,)), ((), ())), preferred_element_type=f32)

    def to_row(column):
        return jnp.transpose(jnp.broadcast_to(column, (128, 128)))[0:1, :]

    def to_lanes(row):
        return jnp.transpose(jnp.broadcast_to(row, (128, 128)))

    def kernel(
        tok, gain, left, right, cot,
        mixer, gtok, gleft, gright, ggain,
        send_a, send_b, cot_in, pre_in, gp_in, mix_in,
        perm, regroup, back_w, fwd_w,
        flat, act, slope, act_q, gm_q, gn,
        inv, corr, stat_out, stat_in, corr_out, corr_in,
        ssem, rsem, stat_ssem, stat_rsem,
    ):
        me = lax.axis_index("blk")

        def peer(i):
            off = n // 2 + i
            off = off + off // n
            return lax.rem(me + off, n)

        barrier = pltpu.get_barrier_semaphore()

        def greet(i, c):
            pl.semaphore_signal(barrier, inc=1, device_id={"blk": peer(i)})
            return c

        lax.fori_loop(0, n - 1, greet, 0)

        def fill(ref, count, test):
            def body(i, c):
                r = lax.broadcasted_iota(jnp.int32, (128, ref.shape[1]), 0) + i * 128
                q = lax.broadcasted_iota(jnp.int32, (128, ref.shape[1]), 1)
                ref[pl.ds(pl.multiple_of(i * 128, 128), 128), :] = jnp.where(test(r, q), 1.0, 0.0).astype(bf16)
                return c

            lax.fori_loop(0, count // 128, body, 0)

        def push(out, into, which, k):
            def body(i, c):
                to = peer(i)
                pltpu.make_async_remote_copy(
                    src_ref=out.at[k, to],
                    dst_ref=into.at[k, me],
                    send_sem=ssem.at[which, k],
                    recv_sem=rsem.at[which, k],
                    device_id={"blk": to},
                ).start()
                return c

            lax.fori_loop(0, n - 1, body, 0)

        def landed(into, which, k):
            span = into.at[k, pl.ds(0, n - 1)]
            pltpu.make_async_copy(span, span, rsem.at[which, k]).wait()

        def sent(out, which, k):
            span = out.at[k, pl.ds(0, n - 1)]
            pltpu.make_async_copy(span, span, ssem.at[which, k]).wait()

        def push_stat(out, into, which):
            def body(i, c):
                pltpu.make_async_remote_copy(
                    src_ref=out,
                    dst_ref=into.at[me],
                    send_sem=stat_ssem.at[which],
                    recv_sem=stat_rsem.at[which],
                    device_id={"blk": peer(i)},
                ).start()
                return c

            into[me] = out[...]
            lax.fori_loop(0, n - 1, body, 0)

        def stat_landed(into, which):
            span = into.at[pl.ds(0, n - 1)]
            pltpu.make_async_copy(span, span, stat_rsem.at[which]).wait()

        def stat_sent(into, which):
            span = into.at[pl.ds(0, n - 1)]
            pltpu.make_async_copy(span, span, stat_ssem.at[which]).wait()

        def rows_of(k):
            return pl.ds(pl.multiple_of(k * tc, tc), tc)

        def put(out, into, k, i, value):
            out[k, pl.ds(i * pieces_in_part, pieces_in_part)] = value.astype(bf16).reshape(
                pieces_in_part, piece, tc
            )

        def scatter(natural, out, into, k):
            def body(i, c):
                block = perm[pl.ds(pl.multiple_of(i * part, part), part), :]
                put(out, into, k, i, nt(block, natural()))
                return c

            lax.fori_loop(0, feats // part, body, 0)

        def own(out, into, k):
            into[k, me] = out[k, me]

        fill(perm, feats, lambda r, q: q == (r & low) * order + (r >> lg))

        stat_out[...] = jnp.zeros_like(stat_out)
        for s in range(strips):
            x = tok[s * 128 : (s + 1) * 128, :].astype(f32)
            stat_out[s : s + 1, :] = to_row(jnp.sum(x * x, axis=1, keepdims=True))
        pl.semaphore_wait(barrier, n - 1)
        push_stat(stat_out, stat_in, 0)

        def cot_step(k, c):
            scatter(lambda: cot[rows_of(k), :], send_a, cot_in, k)
            push(send_a, cot_in, 0, k)
            own(send_a, cot_in, k)
            return c

        lax.fori_loop(0, chunks, cot_step, 0)

        stat_landed(stat_in, 0)
        total = jnp.sum(stat_in[...], axis=0)
        for s in range(strips):
            inv[s * 128 : (s + 1) * 128, :] = lax.rsqrt(to_lanes(total[s : s + 1, :]) / width + epsilon)

        def normed_block(k, b):
            cols = pl.ds(pl.multiple_of(b * order, order), order)
            x = tok[rows_of(k), cols].astype(f32)
            return (x * inv[rows_of(k), :] * gain[:, cols]).astype(bf16)

        def pre_step(k, c):
            def body(b, c):
                cols = pl.ds(pl.multiple_of(b * order, order), order)
                flat[:, cols] = nn(normed_block(k, b), left[b]).astype(bf16)
                return c

            lax.fori_loop(0, local, body, 0)
            scatter(lambda: flat[...], send_b, pre_in, k)
            push(send_b, pre_in, 1, k)
            own(send_b, pre_in, k)
            return c

        lax.fori_loop(0, chunks, pre_step, 0)

        fill(
            regroup,
            feats,
            lambda q, r: q == ((r >> lg) & low) * order + (r >> (2 * lg)) * local + (r & low),
        )

        def expand_step(i, c):
            rs = pl.ds(pl.multiple_of(i * 128, 128), 128)
            r = lax.broadcasted_iota(jnp.int32, (128, order), 0) + i * 128
            y = lax.broadcasted_iota(jnp.int32, (128, order), 1)
            pick = jnp.where(y == (r >> (2 * lg)) * local + (r & low), 1.0, 0.0).astype(bf16)
            for j in range(local):
                cols = slice(j * order, (j + 1) * order)
                here = ((r >> lg) & low) == j
                back_w[rs, cols] = jnp.where(here, nn(pick, right[j]), 0.0).astype(bf16)
                fwd_w[rs, cols] = jnp.where(here, nt(pick, right[j]), 0.0).astype(bf16)
            return c

        lax.fori_loop(0, feats // 128, expand_step, 0)
        gleft[...] = jnp.zeros_like(gleft)
        gright[...] = jnp.zeros_like(gright)
        ggain[...] = jnp.zeros_like(ggain)

        def middle_step(k, c):
            landed(cot_in, 0, k)
            landed(pre_in, 1, k)

            def gelu(i, c):
                rs = pl.ds(pl.multiple_of(i * part, part), part)
                v = pre_in[k, pl.ds(i * pieces_in_part, pieces_in_part)].reshape(part, tc).astype(f32)
                half = 0.5 * (1.0 + lax.erf(v * 0.7071067811865476))
                act[rs, :] = (v * half).astype(bf16)
                slope[rs, :] = half + v * jnp.exp(-0.5 * v * v) * 0.3989422804014327
                return c

            lax.fori_loop(0, feats // part, gelu, 0)

            def group(i, c):
                rs = pl.ds(pl.multiple_of(i * part, part), part)
                block = regroup[rs, :]
                act_q[rs, :] = nn(block, act[...]).astype(bf16)
                gm_q[rs, :] = nn(block, cot_in[k].reshape(feats, tc)).astype(bf16)
                return c

            lax.fori_loop(0, feats // part, group, 0)
            sent(send_b, 1, k)

            def grad(i, c):
                rs = pl.ds(pl.multiple_of(i * part, part), part)
                put(send_b, gp_in, k, i, nn(back_w[rs, :], gm_q[...]) * slope[rs, :])
                return c

            lax.fori_loop(0, feats // part, grad, 0)
            push(send_b, gp_in, 2, k)
            own(send_b, gp_in, k)
            sent(send_a, 0, k)

            def mix(i, c):
                rs = pl.ds(pl.multiple_of(i * part, part), part)
                put(send_a, mix_in, k, i, nn(fwd_w[rs, :], act_q[...]))
                return c

            lax.fori_loop(0, feats // part, mix, 0)
            push(send_a, mix_in, 3, k)
            own(send_a, mix_in, k)

            def factor(j, c):
                rs = pl.ds(pl.multiple_of(j * order, order), order)
                gright[j] += nt(act_q[rs, :], gm_q[rs, :])
                return c

            lax.fori_loop(0, local, factor, 0)
            return c

        lax.fori_loop(0, chunks, middle_step, 0)

        corr_out[...] = jnp.zeros_like(corr_out)

        def turn(into, k):
            for s in range(tc // 128):
                flat[s * 128 : (s + 1) * 128, :] = jnp.transpose(
                    into[k, :, :, s * 128 : (s + 1) * 128].reshape(feats, 128)
                )

        def last_step(k, c):
            landed(gp_in, 2, k)
            turn(gp_in, k)

            def body(b, total):
                cols = pl.ds(pl.multiple_of(b * order, order), order)
                g = nn(flat[...], perm[:, cols]).astype(bf16)
                grad = nt(g, left[b])
                gn[rows_of(k), cols] = grad
                gleft[b] += tn(normed_block(k, b), g)
                x = tok[rows_of(k), cols].astype(f32)
                gx = grad * x
                ggain[:, cols] += jnp.sum(gx * inv[rows_of(k), :], axis=0, keepdims=True)
                return total + gx * gain[:, cols]

            corr[rows_of(k), :] = lax.fori_loop(0, local, body, jnp.zeros((tc, order), f32))
            return c

        lax.fori_loop(0, chunks, last_step, 0)
        for s in range(strips):
            corr_out[s : s + 1, :] = to_row(
                jnp.sum(corr[s * 128 : (s + 1) * 128, :], axis=1, keepdims=True)
            )
        push_stat(corr_out, corr_in, 1)

        def out_step(k, c):
            landed(mix_in, 3, k)
            turn(mix_in, k)

            def body(b, c):
                cols = pl.ds(pl.multiple_of(b * part, part), part)
                mixer[rows_of(k), cols] = nn(flat[...], perm[:, cols]).astype(bf16)
                return c

            lax.fori_loop(0, feats // part, body, 0)
            return c

        early = max(chunks - 2, 0)
        lax.fori_loop(0, early, out_step, 0)

        stat_landed(corr_in, 1)
        total = jnp.sum(corr_in[...], axis=0)
        for s in range(strips):
            rs = slice(s * 128, (s + 1) * 128)
            r = inv[rs, :]
            corr[rs, :] = r * r * r * to_lanes(total[s : s + 1, :]) / width

        def token_step(k, c):
            def body(b, c):
                cols = pl.ds(pl.multiple_of(b * order, order), order)
                x = tok[rows_of(k), cols].astype(f32)
                scaled = gn[rows_of(k), cols] * gain[:, cols]
                gtok[rows_of(k), cols] = (
                    inv[rows_of(k), :] * scaled - x * corr[rows_of(k), :]
                ).astype(bf16)
                return c

            lax.fori_loop(0, local, body, 0)
            return c

        lax.fori_loop(0, chunks, token_step, 0)
        lax.fori_loop(early, chunks, out_step, 0)

        def drain(k, c):
            sent(send_b, 2, k)
            sent(send_a, 3, k)
            return c

        lax.fori_loop(0, chunks, drain, 0)
        stat_sent(stat_in, 0)
        stat_sent(corr_in, 1)

    exchange = pltpu.VMEM((chunks, n, piece, tc), bf16)
    square = pltpu.VMEM((feats, feats), bf16)
    stat_rows = -(-strips // 8) * 8
    vmem = pl.BlockSpec(memory_space=pltpu.VMEM)
    outs = pl.pallas_call(
        kernel,
        out_shape=(
            jax.ShapeDtypeStruct((rows, feats), bf16),
            jax.ShapeDtypeStruct((rows, feats), bf16),
            jax.ShapeDtypeStruct((local, order, order), f32),
            jax.ShapeDtypeStruct((local, order, order), f32),
            jax.ShapeDtypeStruct((1, feats), f32),
        ),
        in_specs=[vmem] * 5,
        out_specs=(vmem,) * 5,
        scratch_shapes=[exchange] * 6
        + [square] * 4
        + [
            pltpu.VMEM((tc, feats), bf16),
            pltpu.VMEM((feats, tc), bf16),
            pltpu.VMEM((feats, tc), f32),
            pltpu.VMEM((feats, tc), bf16),
            pltpu.VMEM((feats, tc), bf16),
            pltpu.VMEM((rows, feats), f32),
            pltpu.VMEM((rows, 128), f32),
            pltpu.VMEM((rows, 128), f32),
            pltpu.VMEM((stat_rows, 128), f32),
            pltpu.VMEM((n, stat_rows, 128), f32),
            pltpu.VMEM((stat_rows, 128), f32),
            pltpu.VMEM((n, stat_rows, 128), f32),
            pltpu.SemaphoreType.DMA((4, chunks)),
            pltpu.SemaphoreType.DMA((4, chunks)),
            pltpu.SemaphoreType.DMA((2,)),
            pltpu.SemaphoreType.DMA((2,)),
        ],
        compiler_params=pltpu.CompilerParams(
            collective_id=0, has_side_effects=True, vmem_limit_bytes=60 * 1024 * 1024
        ),
        cost_estimate=pl.CostEstimate(
            flops=20 * rows * feats * feats, bytes_accessed=8 * rows * feats, transcendentals=2 * rows * feats
        ),
        name="monarch",
    )(tokens, norm_gain.astype(f32).reshape(1, feats), left_factor, right_factor, cotangent)
    return (*outs[:4], outs[4].reshape(feats))


def solution(mesh):
    placed = (
        P("groups", "blk"),
        P("blk"),
        P("blk", None, None),
        P("blk", None, None),
        P("groups", "blk"),
    )
    n = mesh.shape["blk"]

    def body(tokens, norm_gain, left_factor, right_factor, cotangent):
        rows, feats = tokens.shape
        local, order = left_factor.shape[0], left_factor.shape[1]
        fits = (
            n > 1
            and local & (local - 1) == 0
            and (local * local) % 16 == 0
            and 256 % (local * local) == 0
            and order == 128
            and n * local == order
            and right_factor.shape == left_factor.shape
            and rows % CHUNK == 0
            and feats % 256 == 0
        )
        if fits:
            return fast(n, n * feats, tokens, norm_gain, left_factor, right_factor, cotangent)
        return on_device(n * feats, tokens, norm_gain, left_factor, right_factor, cotangent)

    return jax.shard_map(
        body,
        mesh=mesh,
        in_specs=placed,
        out_specs=(
            P("groups", "blk"),
            P("groups", "blk"),
            P(("groups", "blk"), None, None),
            P(("groups", "blk"), None, None),
            P(("groups", "blk")),
        ),
        check_vma=False,
    )
```

```python
import jax
import jax.numpy as jnp
from jax import lax
from jax.experimental import pallas as pl
from jax.experimental.pallas import tpu as pltpu
from jax.sharding import PartitionSpec as P

CHUNK = 256


epsilon = 1e-06


def gelu_slope(inputs_f):
    return (
        0.5 * (1.0 + lax.erf(inputs_f * 0.7071067811865476))
        + inputs_f * jnp.exp(-0.5 * inputs_f * inputs_f) * 0.3989422804014327
    )


def on_device(width, tokens, norm_gain, left_factor, right_factor, cotangent):
    row_count = tokens.shape[0]
    local_blocks = left_factor.shape[0]
    block_order = left_factor.shape[1]
    widened = tokens.astype(jnp.float32)
    square_sum = lax.psum(jnp.sum(widened * widened, axis=1), "blk")
    inverse_rms = lax.rsqrt(square_sum / width + epsilon)
    gain_wide = norm_gain.astype(jnp.float32)
    normed = (widened * inverse_rms[:, None] * gain_wide[None, :]).astype(jnp.bfloat16)
    blocks = normed.reshape(row_count, local_blocks, block_order)
    pre_act = jnp.einsum(
        "tbi,bij->btj", blocks, left_factor, preferred_element_type=jnp.float32
    ).astype(jnp.bfloat16)
    pre_piece = lax.all_to_all(pre_act, "blk", split_axis=2, concat_axis=0, tiled=True)
    active = jax.nn.gelu(pre_piece.astype(jnp.float32), approximate=False).astype(jnp.bfloat16)
    mixed_out = jnp.einsum(
        "btj,jbc->jtc", active, right_factor, preferred_element_type=jnp.float32
    ).astype(jnp.bfloat16)
    mixed_out = lax.all_to_all(mixed_out, "blk", split_axis=2, concat_axis=0, tiled=True)
    incoming = jnp.transpose(cotangent.reshape(row_count, -1, block_order), (1, 0, 2))
    grad_mixed = lax.all_to_all(incoming, "blk", split_axis=2, concat_axis=0, tiled=True)
    mixer_out = jnp.transpose(mixed_out, (1, 2, 0)).reshape(row_count, -1)
    grad_right = jnp.einsum("btj,ctj->jbc", active, grad_mixed, preferred_element_type=jnp.float32)
    grad_act = jnp.einsum(
        "ctj,jbc->btj", grad_mixed, right_factor, preferred_element_type=jnp.float32
    )
    grad_pre = (grad_act * gelu_slope(pre_piece.astype(jnp.float32))).astype(jnp.bfloat16)
    grad_back = lax.all_to_all(grad_pre, "blk", split_axis=0, concat_axis=2, tiled=True)
    grad_left = jnp.einsum("tbi,btj->bij", blocks, grad_back, preferred_element_type=jnp.float32)
    grad_normed = jnp.einsum(
        "btj,bij->tbi", grad_back, left_factor, preferred_element_type=jnp.float32
    ).reshape(row_count, -1)
    grad_gain = jnp.sum(grad_normed * widened * inverse_rms[:, None], axis=0)
    scaled = grad_normed * gain_wide[None, :]
    correction = lax.psum(jnp.sum(scaled * widened, axis=1), "blk")
    grad_tokens = (
        inverse_rms[:, None] * scaled - widened * (inverse_rms**3 * correction / width)[:, None]
    ).astype(jnp.bfloat16)
    return (mixer_out, grad_tokens, grad_left, grad_right, grad_gain)

def hand_over(arrays, pieces):
    count = len(arrays)

    def kernel(*refs):
        held, taken, given = refs[2 * count : 3 * count], refs[-2], refs[-1]
        copies = []
        for i in range(count):
            rows = arrays[i].shape[0]
            parts = pieces if rows % (pieces * 16) == 0 else 1
            step = rows // parts
            for p in range(parts):
                span = pl.ds(p * step, step)
                inward = pltpu.make_async_copy(refs[i].at[span], held[i].at[span], taken.at[i, p])
                outward = pltpu.make_async_copy(
                    held[i].at[span], refs[count + i].at[span], given.at[i, p]
                )
                copies.append((inward, outward))
        for inward, outward in copies:
            inward.start()
        for inward, outward in copies:
            inward.wait()
            outward.start()
        for inward, outward in copies:
            outward.wait()

    anywhere = pl.BlockSpec(memory_space=pl.ANY)
    return pl.pallas_call(
        kernel,
        out_shape=tuple(jax.ShapeDtypeStruct(a.shape, a.dtype) for a in arrays),
        in_specs=[anywhere] * count,
        out_specs=(anywhere,) * count,
        scratch_shapes=[pltpu.VMEM(a.shape, a.dtype) for a in arrays]
        + [pltpu.SemaphoreType.DMA((count, pieces))] * 2,
        compiler_params=pltpu.CompilerParams(vmem_limit_bytes=60 * 1024 * 1024),
        name="hand_over",
    )(*arrays)


def fast(n, width, tokens, norm_gain, left_factor, right_factor, cotangent):
    rows = tokens.shape[0]
    feats = tokens.shape[1]
    local, order = left_factor.shape[0], left_factor.shape[1]
    piece = local * local
    lg = local.bit_length() - 1
    low = local - 1
    tc = CHUNK
    chunks = rows // tc
    strips = rows // 128
    f32, bf16 = jnp.float32, jnp.bfloat16
    part = 256
    pieces_in_part = part // piece

    def nn(a, b):
        return lax.dot_general(a, b, (((1,), (0,)), ((), ())), preferred_element_type=f32)

    def nt(a, b):
        return lax.dot_general(a, b, (((1,), (1,)), ((), ())), preferred_element_type=f32)

    def tn(a, b):
        return lax.dot_general(a, b, (((0,), (0,)), ((), ())), preferred_element_type=f32)

    def to_row(column):
        return jnp.transpose(jnp.broadcast_to(column, (128, 128)))[0:1, :]

    def to_lanes(row):
        return jnp.transpose(jnp.broadcast_to(row, (128, 128)))

    def kernel(
        tok_hbm, gain, left, right, cot_hbm,
        mixer_hbm, gtok_hbm, gleft_hbm, gright_hbm, ggain,
        tok, cot, gleft, gright,
        send_a, send_b, cot_in, pre_in, gp_in, mix_in,
        perm, regroup, back_w, fwd_w,
        flat, act, slope, act_q, gm_q, gn,
        inv, corr, stat_out, stat_in, corr_out, corr_in,
        ssem, rsem, stat_ssem, stat_rsem, load_sem, tok_sem, mix_sem, gtok_sem, grad_sem,
    ):
        me = lax.axis_index("blk")

        def rows_of(k):
            return pl.ds(pl.multiple_of(k * tc, tc), tc)

        def peer(i):
            off = n // 2 + i
            off = off + off // n
            return lax.rem(me + off, n)

        barrier = pltpu.get_barrier_semaphore()

        def greet(i, c):
            pl.semaphore_signal(barrier, inc=1, device_id={"blk": peer(i)})
            return c

        lax.fori_loop(0, n - 1, greet, 0)

        def load(k):
            return pltpu.make_async_copy(cot_hbm.at[rows_of(k)], cot.at[rows_of(k)], load_sem.at[k])

        def load_start(k, c):
            load(k).start()
            return c

        lax.fori_loop(0, chunks, load_start, 0)
        load_tok = pltpu.make_async_copy(tok_hbm, tok, tok_sem)
        load_tok.start()

        def fill(ref, count, test):
            def body(i, c):
                r = lax.broadcasted_iota(jnp.int32, (128, ref.shape[1]), 0) + i * 128
                q = lax.broadcasted_iota(jnp.int32, (128, ref.shape[1]), 1)
                ref[pl.ds(pl.multiple_of(i * 128, 128), 128), :] = jnp.where(test(r, q), 1.0, 0.0).astype(bf16)
                return c

            lax.fori_loop(0, count // 128, body, 0)

        def push(out, into, which, k):
            def body(i, c):
                to = peer(i)
                pltpu.make_async_remote_copy(
                    src_ref=out.at[k, to],
                    dst_ref=into.at[k, me],
                    send_sem=ssem.at[which, k],
                    recv_sem=rsem.at[which, k],
                    device_id={"blk": to},
                ).start()
                return c

            lax.fori_loop(0, n - 1, body, 0)

        def landed(into, which, k):
            span = into.at[k, pl.ds(0, n - 1)]
            pltpu.make_async_copy(span, span, rsem.at[which, k]).wait()

        def sent(out, which, k):
            span = out.at[k, pl.ds(0, n - 1)]
            pltpu.make_async_copy(span, span, ssem.at[which, k]).wait()

        def push_stat(out, into, which):
            def body(i, c):
                pltpu.make_async_remote_copy(
                    src_ref=out,
                    dst_ref=into.at[me],
                    send_sem=stat_ssem.at[which],
                    recv_sem=stat_rsem.at[which],
                    device_id={"blk": peer(i)},
                ).start()
                return c

            into[me] = out[...]
            lax.fori_loop(0, n - 1, body, 0)

        def stat_landed(into, which):
            span = into.at[pl.ds(0, n - 1)]
            pltpu.make_async_copy(span, span, stat_rsem.at[which]).wait()

        def stat_sent(into, which):
            span = into.at[pl.ds(0, n - 1)]
            pltpu.make_async_copy(span, span, stat_ssem.at[which]).wait()

        def put(out, into, k, i, value):
            out[k, pl.ds(i * pieces_in_part, pieces_in_part)] = value.astype(bf16).reshape(
                pieces_in_part, piece, tc
            )

        def scatter(natural, out, into, k):
            def body(i, c):
                block = perm[pl.ds(pl.multiple_of(i * part, part), part), :]
                put(out, into, k, i, nt(block, natural()))
                return c

            lax.fori_loop(0, feats // part, body, 0)

        def own(out, into, k):
            into[k, me] = out[k, me]

        fill(perm, feats, lambda r, q: q == (r & low) * order + (r >> lg))

        def cot_step(k, c):
            load(k).wait()
            scatter(lambda: cot[rows_of(k), :], send_a, cot_in, k)
            push(send_a, cot_in, 0, k)
            own(send_a, cot_in, k)
            return c

        pl.semaphore_wait(barrier, n - 1)
        cot_step(0, 0)
        load_tok.wait()
        stat_out[...] = jnp.zeros_like(stat_out)
        for s in range(strips):
            x = tok[s * 128 : (s + 1) * 128, :].astype(f32)
            stat_out[s : s + 1, :] = to_row(jnp.sum(x * x, axis=1, keepdims=True))
        push_stat(stat_out, stat_in, 0)

        lax.fori_loop(1, chunks, cot_step, 0)

        stat_landed(stat_in, 0)
        total = jnp.sum(stat_in[...], axis=0)
        for s in range(strips):
            inv[s * 128 : (s + 1) * 128, :] = lax.rsqrt(to_lanes(total[s : s + 1, :]) / width + epsilon)

        def normed_block(k, b):
            cols = pl.ds(pl.multiple_of(b * order, order), order)
            x = tok[rows_of(k), cols].astype(f32)
            return (x * inv[rows_of(k), :] * gain[:, cols]).astype(bf16)

        def pre_step(k, c):
            def body(b, c):
                cols = pl.ds(pl.multiple_of(b * order, order), order)
                flat[:, cols] = nn(normed_block(k, b), left[b]).astype(bf16)
                return c

            lax.fori_loop(0, local, body, 0)
            scatter(lambda: flat[...], send_b, pre_in, k)
            push(send_b, pre_in, 1, k)
            own(send_b, pre_in, k)
            return c

        lax.fori_loop(0, chunks, pre_step, 0)

        fill(
            regroup,
            feats,
            lambda q, r: q == ((r >> lg) & low) * order + (r >> (2 * lg)) * local + (r & low),
        )

        def expand_step(i, c):
            rs = pl.ds(pl.multiple_of(i * 128, 128), 128)
            r = lax.broadcasted_iota(jnp.int32, (128, order), 0) + i * 128
            y = lax.broadcasted_iota(jnp.int32, (128, order), 1)
            pick = jnp.where(y == (r >> (2 * lg)) * local + (r & low), 1.0, 0.0).astype(bf16)
            for j in range(local):
                cols = slice(j * order, (j + 1) * order)
                here = ((r >> lg) & low) == j
                back_w[rs, cols] = jnp.where(here, nn(pick, right[j]), 0.0).astype(bf16)
                fwd_w[rs, cols] = jnp.where(here, nt(pick, right[j]), 0.0).astype(bf16)
            return c

        lax.fori_loop(0, feats // 128, expand_step, 0)
        gleft[...] = jnp.zeros_like(gleft)
        gright[...] = jnp.zeros_like(gright)
        ggain[...] = jnp.zeros_like(ggain)

        def middle_step(k, c):
            landed(cot_in, 0, k)
            landed(pre_in, 1, k)

            def gelu(i, c):
                rs = pl.ds(pl.multiple_of(i * part, part), part)
                v = pre_in[k, pl.ds(i * pieces_in_part, pieces_in_part)].reshape(part, tc).astype(f32)
                half = 0.5 * (1.0 + lax.erf(v * 0.7071067811865476))
                act[rs, :] = (v * half).astype(bf16)
                slope[rs, :] = half + v * jnp.exp(-0.5 * v * v) * 0.3989422804014327
                return c

            lax.fori_loop(0, feats // part, gelu, 0)

            def group(i, c):
                rs = pl.ds(pl.multiple_of(i * part, part), part)
                block = regroup[rs, :]
                act_q[rs, :] = nn(block, act[...]).astype(bf16)
                gm_q[rs, :] = nn(block, cot_in[k].reshape(feats, tc)).astype(bf16)
                return c

            lax.fori_loop(0, feats // part, group, 0)
            sent(send_b, 1, k)

            def grad(i, c):
                rs = pl.ds(pl.multiple_of(i * part, part), part)
                put(send_b, gp_in, k, i, nn(back_w[rs, :], gm_q[...]) * slope[rs, :])
                return c

            lax.fori_loop(0, feats // part, grad, 0)
            push(send_b, gp_in, 2, k)
            own(send_b, gp_in, k)
            sent(send_a, 0, k)

            def mix(i, c):
                rs = pl.ds(pl.multiple_of(i * part, part), part)
                put(send_a, mix_in, k, i, nn(fwd_w[rs, :], act_q[...]))
                return c

            lax.fori_loop(0, feats // part, mix, 0)
            own(send_a, mix_in, k)

            def factor(j, c):
                rs = pl.ds(pl.multiple_of(j * order, order), order)
                gright[j] += nt(act_q[rs, :], gm_q[rs, :])
                return c

            lax.fori_loop(0, local, factor, 0)
            return c

        lax.fori_loop(0, chunks, middle_step, 0)
        copy_right = pltpu.make_async_copy(gright, gright_hbm, grad_sem.at[1])
        copy_right.start()
        early = max(chunks - 2, 0)

        def push_mix(k, c):
            push(send_a, mix_in, 3, k)
            return c

        lax.fori_loop(0, early, push_mix, 0)

        corr_out[...] = jnp.zeros_like(corr_out)

        def turn(into, k):
            for s in range(tc // 128):
                flat[s * 128 : (s + 1) * 128, :] = jnp.transpose(
                    into[k, :, :, s * 128 : (s + 1) * 128].reshape(feats, 128)
                )

        def last_step(k, c):
            landed(gp_in, 2, k)
            turn(gp_in, k)

            def body(b, total):
                cols = pl.ds(pl.multiple_of(b * order, order), order)
                g = nn(flat[...], perm[:, cols]).astype(bf16)
                grad = nt(g, left[b])
                gn[rows_of(k), cols] = grad
                gleft[b] += tn(normed_block(k, b), g)
                x = tok[rows_of(k), cols].astype(f32)
                gx = grad * x
                ggain[:, cols] += jnp.sum(gx * inv[rows_of(k), :], axis=0, keepdims=True)
                return total + gx * gain[:, cols]

            corr[rows_of(k), :] = lax.fori_loop(0, local, body, jnp.zeros((tc, order), f32))
            return c

        lax.fori_loop(0, chunks, last_step, 0)
        for s in range(strips):
            corr_out[s : s + 1, :] = to_row(
                jnp.sum(corr[s * 128 : (s + 1) * 128, :], axis=1, keepdims=True)
            )
        push_stat(corr_out, corr_in, 1)
        lax.fori_loop(early, chunks, push_mix, 0)
        copy_left = pltpu.make_async_copy(gleft, gleft_hbm, grad_sem.at[0])
        copy_left.start()

        def store_mix(k):
            return pltpu.make_async_copy(cot.at[rows_of(k)], mixer_hbm.at[rows_of(k)], mix_sem.at[k])

        def store_tok(k):
            return pltpu.make_async_copy(tok.at[rows_of(k)], gtok_hbm.at[rows_of(k)], gtok_sem.at[k])

        def out_step(k, c):
            landed(mix_in, 3, k)
            turn(mix_in, k)

            def body(b, c):
                cols = pl.ds(pl.multiple_of(b * part, part), part)
                cot[rows_of(k), cols] = nn(flat[...], perm[:, cols]).astype(bf16)
                return c

            lax.fori_loop(0, feats // part, body, 0)
            store_mix(k).start()
            return c

        lax.fori_loop(0, early, out_step, 0)

        stat_landed(corr_in, 1)
        total = jnp.sum(corr_in[...], axis=0)
        for s in range(strips):
            rs = slice(s * 128, (s + 1) * 128)
            r = inv[rs, :]
            corr[rs, :] = r * r * r * to_lanes(total[s : s + 1, :]) / width

        def token_step(k, c):
            def body(b, c):
                cols = pl.ds(pl.multiple_of(b * order, order), order)
                x = tok[rows_of(k), cols].astype(f32)
                scaled = gn[rows_of(k), cols] * gain[:, cols]
                tok[rows_of(k), cols] = (
                    inv[rows_of(k), :] * scaled - x * corr[rows_of(k), :]
                ).astype(bf16)
                return c

            lax.fori_loop(0, local, body, 0)
            store_tok(k).start()
            return c

        lax.fori_loop(0, chunks, token_step, 0)
        lax.fori_loop(early, chunks, out_step, 0)

        def drain(k, c):
            sent(send_b, 2, k)
            sent(send_a, 3, k)
            store_mix(k).wait()
            store_tok(k).wait()
            return c

        lax.fori_loop(0, chunks, drain, 0)
        stat_sent(stat_in, 0)
        stat_sent(corr_in, 1)
        copy_left.wait()
        copy_right.wait()

    exchange = pltpu.VMEM((chunks, n, piece, tc), bf16)
    square = pltpu.VMEM((feats, feats), bf16)
    stat_rows = -(-strips // 8) * 8
    vmem = pl.BlockSpec(memory_space=pltpu.VMEM)
    anywhere = pl.BlockSpec(memory_space=pl.ANY)
    outs = pl.pallas_call(
        kernel,
        out_shape=(
            jax.ShapeDtypeStruct((rows, feats), bf16),
            jax.ShapeDtypeStruct((rows, feats), bf16),
            jax.ShapeDtypeStruct((local, order, order), f32),
            jax.ShapeDtypeStruct((local, order, order), f32),
            jax.ShapeDtypeStruct((1, feats), f32),
        ),
        in_specs=[anywhere, vmem, vmem, vmem, anywhere],
        out_specs=(anywhere,) * 4 + (vmem,),
        scratch_shapes=[pltpu.VMEM((rows, feats), bf16)] * 2
        + [pltpu.VMEM((local, order, order), f32)] * 2
        + [exchange] * 6
        + [square] * 4
        + [
            pltpu.VMEM((tc, feats), bf16),
            pltpu.VMEM((feats, tc), bf16),
            pltpu.VMEM((feats, tc), f32),
            pltpu.VMEM((feats, tc), bf16),
            pltpu.VMEM((feats, tc), bf16),
            pltpu.VMEM((rows, feats), f32),
            pltpu.VMEM((rows, 128), f32),
            pltpu.VMEM((rows, 128), f32),
            pltpu.VMEM((stat_rows, 128), f32),
            pltpu.VMEM((n, stat_rows, 128), f32),
            pltpu.VMEM((stat_rows, 128), f32),
            pltpu.VMEM((n, stat_rows, 128), f32),
            pltpu.SemaphoreType.DMA((4, chunks)),
            pltpu.SemaphoreType.DMA((4, chunks)),
            pltpu.SemaphoreType.DMA((2,)),
            pltpu.SemaphoreType.DMA((2,)),
            pltpu.SemaphoreType.DMA((chunks,)),
            pltpu.SemaphoreType.DMA,
            pltpu.SemaphoreType.DMA((chunks,)),
            pltpu.SemaphoreType.DMA((chunks,)),
            pltpu.SemaphoreType.DMA((2,)),
        ],
        compiler_params=pltpu.CompilerParams(
            collective_id=0, has_side_effects=True, vmem_limit_bytes=60 * 1024 * 1024
        ),
        cost_estimate=pl.CostEstimate(
            flops=20 * rows * feats * feats, bytes_accessed=8 * rows * feats, transcendentals=2 * rows * feats
        ),
        name="monarch",
    )(tokens, norm_gain.astype(f32).reshape(1, feats), left_factor, right_factor, cotangent)
    outs = hand_over(outs, chunks)
    return (*outs[:4], outs[4].reshape(feats))


def solution(mesh):
    placed = (
        P("groups", "blk"),
        P("blk"),
        P("blk", None, None),
        P("blk", None, None),
        P("groups", "blk"),
    )
    n = mesh.shape["blk"]

    def body(tokens, norm_gain, left_factor, right_factor, cotangent):
        rows, feats = tokens.shape
        local, order = left_factor.shape[0], left_factor.shape[1]
        fits = (
            n > 1
            and local & (local - 1) == 0
            and (local * local) % 16 == 0
            and 256 % (local * local) == 0
            and order == 128
            and n * local == order
            and right_factor.shape == left_factor.shape
            and rows % CHUNK == 0
            and feats % 256 == 0
        )
        if fits:
            return fast(n, n * feats, tokens, norm_gain, left_factor, right_factor, cotangent)
        return on_device(n * feats, tokens, norm_gain, left_factor, right_factor, cotangent)

    return jax.shard_map(
        body,
        mesh=mesh,
        in_specs=placed,
        out_specs=(
            P("groups", "blk"),
            P("groups", "blk"),
            P(("groups", "blk"), None, None),
            P(("groups", "blk"), None, None),
            P(("groups", "blk")),
        ),
        check_vma=False,
    )
```
